256 devices in a mesh: seq: 2 (over y_lo), ctx: 4 (over x), head: 32 (over z, y_hi, core).
Axes of the slice: x: 4, y: 4 (y_hi: 2, y_lo: 2; y = y_hi * 2 + y_lo), z: 8, core: 2. Of those that a mesh axis runs over, the one named last changes fastest.
Arguments:
- queries: bfloat16 [4, 2048, 2, 32, 128], P('ctx', ('seq', 'head')), may hold values from -8 to 8
- key_states: bfloat16 [4, 2048, 2, 32, 128], P('ctx', ('seq', 'head')), may hold values from -6 to 6
- value_states: bfloat16 [4, 2048, 2, 32, 128], P('ctx', ('seq', 'head')), may hold values from -6 to 6
- output_grad: bfloat16 [4, 2048, 2, 32, 128], P('ctx', ('seq', 'head')), may hold values from -6 to 6
Outputs:
- attention_out: bfloat16 [4, 2048, 2, 32, 128], P('ctx', ('seq', 'head'))
- query_grad: bfloat16 [4, 2048, 2, 32, 128], P('ctx', ('seq', 'head'))
- key_grad: bfloat16 [4, 2048, 2, 32, 128], P('ctx', ('seq', 'head'))
- value_grad: bfloat16 [4, 2048, 2, 32, 128], P('ctx', ('seq', 'head'))
The draws below stay inside these ranges and needn't reach their ends.
All inputs are finite; a program needn't handle non-finite values.
Results may differ from the reference program's by a relative error of at most 0.0088.
Values may be sent and summed in bfloat16 or wider, within the bound.
A program may use at most 64 MiB of HBM per device.

```python
import jax
import jax.numpy as jnp
from jax import lax

H = 32
DH = 128
GROUP = 2048
SEQS = 2
GROUPS = 4
SEQLEN = 8192


def draw_queries(key, part):
    key = jax.random.fold_in(key, 3)
    full_shape = (GROUPS, GROUP, SEQS, H, DH)
    values = jnp.clip(jax.random.normal(key, full_shape, jnp.float32), -6.0, 6.0)
    return values.astype(jnp.bfloat16)


def draw_key_states(key, part):
    key = jax.random.fold_in(key, 7)
    full_shape = (GROUPS, GROUP, SEQS, H, DH)
    values = jnp.clip(jax.random.normal(key, full_shape, jnp.float32), -6.0, 6.0)
    return values.astype(jnp.bfloat16)


def block_scale(rng, dims, pieces, smallest, top_value):
    loudness, own = 1.0, jax.random.fold_in(rng, 6)
    for position, blocks in pieces:
        steps = jnp.exp(jax.random.uniform(jax.random.fold_in(own, position), (blocks,), jnp.float32, smallest / len(pieces), top_value / len(pieces)))
        loudness = loudness * jnp.repeat(steps, dims[position] // blocks).reshape([-1 if axis == position else 1 for axis in range(len(dims))])
    return loudness


def scatter_about(own_key, dims, deviation, reach, shards=(), kind=jnp.bfloat16):
    loudness = block_scale(own_key, dims, shards, -0.22, 0.18) if shards else 1.0
    entries = jax.random.normal(own_key, dims, jnp.float32) * deviation * loudness
    return jnp.minimum(jnp.maximum(entries, -reach), reach).astype(kind)


def setup_inputs(seed: int = 0) -> dict:
    key_list = jax.random.split(jax.random.key(seed), 5)
    queries = draw_queries(jax.random.fold_in(key_list[4], 71), 0)
    key_states = draw_key_states(jax.random.fold_in(key_list[4], 71), 0)
    value_states = scatter_about(key_list[2], (GROUPS, GROUP, SEQS, H, DH), 1.0, 6.0, ((0, 4), (1, 64)))
    output_grad = scatter_about(key_list[3], (GROUPS, GROUP, SEQS, H, DH), 1.0, 6.0, ((0, 4), (1, 64)))
    return {"queries": queries, "key_states": key_states, "value_states": value_states, "output_grad": output_grad}


def attend(query_rows, key_rows, value_rows, grad_rows):
    length, head_count, head_width = query_rows.shape
    scaling = head_width ** -0.5
    block_len = min(512, length)
    q_float = query_rows.astype(jnp.float32)
    k_float = key_rows.astype(jnp.float32)
    v_float = value_rows.astype(jnp.float32)
    g_float = grad_rows.astype(jnp.float32)
    key_total = jnp.zeros(key_rows.shape, jnp.float32)
    value_total = jnp.zeros(key_rows.shape, jnp.float32)
    outputs = []
    query_parts = []
    for row_block in range(length // block_len):
        start = row_block * block_len
        limit = start + block_len
        q_part = q_float[start:limit]
        g_part = g_float[start:limit]
        k_part = k_float[:limit]
        v_part = v_float[:limit]
        scores = jnp.einsum("qhd,khd->hqk", q_part, k_part) * scaling
        causal = jnp.arange(limit)[None, :] <= start + jnp.arange(block_len)[:, None]
        scores = jnp.where(causal[None], scores, -jnp.inf)
        largest = jnp.max(scores, axis=2, keepdims=True)
        weights = jnp.exp(scores - largest)
        weights = weights / jnp.sum(weights, axis=2, keepdims=True)
        weights_low = lax.optimization_barrier(weights.astype(jnp.bfloat16)).astype(jnp.float32)
        attended = jnp.einsum("hqk,khd->qhd", weights_low, v_part)
        grad_probs = jnp.einsum("qhd,khd->hqk", g_part, v_part)
        row_dot = jnp.transpose(jnp.sum(g_part * attended, axis=2))[:, :, None]
        grad_scores = weights * (grad_probs - row_dot)
        grad_low = lax.optimization_barrier(grad_scores.astype(jnp.bfloat16)).astype(jnp.float32)
        query_parts.append(jnp.einsum("hqk,khd->qhd", grad_low, k_part) * scaling)
        key_total = key_total.at[:limit].add(jnp.einsum("hqk,qhd->khd", grad_low, q_part) * scaling)
        value_total = value_total.at[:limit].add(jnp.einsum("hqk,qhd->khd", weights_low, g_part))
        outputs.append(attended)
    return (jnp.concatenate(outputs, axis=0).astype(jnp.bfloat16),
            jnp.concatenate(query_parts, axis=0).astype(jnp.bfloat16),
            key_total.astype(jnp.bfloat16),
            value_total.astype(jnp.bfloat16))


def to_items(array):
    sequences = jnp.transpose(array, (2, 0, 1, 3, 4)).reshape(SEQS, SEQLEN, H, DH)
    shifted = jnp.roll(sequences[:, :, H // 2:], -(GROUP // 2), axis=1)
    sequences = jnp.concatenate([sequences[:, :, :H // 2], shifted], axis=2)
    grouped = sequences.reshape(SEQS, GROUPS, GROUP, H, DH)
    return jnp.transpose(grouped, (0, 1, 3, 2, 4)).reshape(SEQS * GROUPS * H, GROUP, 1, DH)


def from_items(items):
    grouped = jnp.transpose(items.reshape(SEQS, GROUPS, H, GROUP, DH), (0, 1, 3, 2, 4))
    sequences = grouped.reshape(SEQS, SEQLEN, H, DH)
    restored = jnp.roll(sequences[:, :, H // 2:], GROUP // 2, axis=1)
    sequences = jnp.concatenate([sequences[:, :, :H // 2], restored], axis=2)
    return jnp.transpose(sequences.reshape(SEQS, GROUPS, GROUP, H, DH), (1, 2, 0, 3, 4))


def run_group(group):
    return attend(group[0], group[1], group[2], group[3])


def reference(queries, key_states, value_states, output_grad):
    items = (to_items(queries), to_items(key_states), to_items(value_states), to_items(output_grad))
    results = lax.map(run_group, items)
    return (from_items(results[0]), from_items(results[1]), from_items(results[2]), from_items(results[3]))
```

```python
import functools
import math

import jax
import jax.numpy as jnp
from jax import lax
from jax.experimental import pallas as pl
from jax.experimental.pallas import tpu as pltpu
from jax.sharding import PartitionSpec as P

H = 32
T = 2048
D = 128
BLOCKS = 64
ROWS = T // BLOCKS
TB = 256
NB = T // TB
SCALE = D**-0.5
EXP2_SCALE = SCALE * math.log2(math.e)
NT = (((1,), (1,)), ((), ()))
NN = (((1,), (0,)), ((), ()))
MESH = pl.DeviceIdType.MESH
IN_GROUPS = ((0, 2), (2, 1), (3, 1))
OUT_GROUPS = ((0, 1), (1, 1), (2, 2))


def dot(a, b, dims=NN):
    return lax.dot_general(a, b, dims, preferred_element_type=jnp.float32)


def tile(i, n=1):
    return pl.ds(i * TB, n * TB)


def rows(block):
    return pl.ds(pl.multiple_of(block * ROWS, ROWS), ROWS)


def softmax_weights(q, k, scores, weights):
    for i in range(NB):
        q_tile = q[tile(i)]
        top = None
        for j in range(i + 1):
            s = dot(k[tile(j)], q_tile, NT)
            if j == i:
                key_pos = lax.broadcasted_iota(jnp.int32, (TB, TB), 0)
                query_pos = lax.broadcasted_iota(jnp.int32, (TB, TB), 1)
                s = jnp.where(key_pos <= query_pos, s, -jnp.inf)
            scores[tile(j)] = s
            part = jnp.max(s, axis=0, keepdims=True)
            top = part if top is None else jnp.maximum(top, part)
        shift = top * EXP2_SCALE
        total = None
        for j in range(i + 1):
            e = jnp.exp2(scores[tile(j)] * EXP2_SCALE - shift)
            scores[tile(j)] = e
            part = jnp.sum(e, axis=0, keepdims=True)
            total = part if total is None else total + part
        inverse = 1.0 / total
        for j in range(i + 1):
            weights[tile(j), tile(i)] = (scores[tile(j)] * inverse).astype(jnp.bfloat16)


def attended(v_t, weights, out, out_wide):
    for i in range(NB):
        o = dot(v_t[:, 0 : (i + 1) * TB], weights[0 : (i + 1) * TB, tile(i)]).T
        out_wide[tile(i)] = o
        out[tile(i)] = o.astype(jnp.bfloat16)


def value_grads(weights, g, dv):
    for j in range(NB):
        n = NB - j
        dv[tile(j)] = dot(weights[tile(j), tile(j, n)], g[tile(j, n)]).astype(jnp.bfloat16)


def row_dots(g, out_wide, row_dot):
    ones = jnp.ones((8, D), jnp.bfloat16)
    for i in range(NB):
        x = g[tile(i)].astype(jnp.float32) * out_wide[tile(i)]
        high = x.astype(jnp.bfloat16)
        low = (x - high.astype(jnp.float32)).astype(jnp.bfloat16)
        row_dot[:, tile(i)] = dot(ones, high, NT) + dot(ones, low, NT)


def score_grads(weights, q, k_t, v, g, row_dot, ds, dq, dk):
    for i in range(NB):
        r = row_dot[0:1, tile(i)]
        for j in range(i + 1):
            dp = dot(v[tile(j)], g[tile(i)], NT)
            w = weights[tile(j), tile(i)].astype(jnp.float32)
            ds[tile(j), tile(i)] = (w * (dp - r)).astype(jnp.bfloat16)
        grad = dot(k_t[:, 0 : (i + 1) * TB], ds[0 : (i + 1) * TB, tile(i)])
        dq[tile(i)] = (grad * SCALE).T.astype(jnp.bfloat16)
    for j in range(NB):
        n = NB - j
        dk[tile(j)] = (dot(ds[tile(j), tile(j, n)], q[tile(j, n)]) * SCALE).astype(jnp.bfloat16)


def kernel(
    q_in, k_in, v_in, g_in, o_out, dq_out, dk_out, dv_out,
    held, sent, items, made, given,
    scores, weights, ds, v_t, k_t, out_wide, row_dot,
    load_sem, store_sem, in_send, in_recv, out_send, out_recv, own_send,
):
    seq = lax.axis_index("seq")
    ctx = lax.axis_index("ctx")
    head = lax.axis_index("head")
    me = seq * 32 + head
    z = head // 4
    y = ((head // 2) % 2) * 2 + seq
    core = head % 2
    shifted_me = head >= H // 2
    local = jnp.logical_or(jnp.logical_not(shifted_me), seq == 1)

    def partner(t):
        e = t // 8
        z2 = (z + 3 * t) % 8
        y2 = (y + e) % 4
        core2 = (core + e // 4) % 2
        return y2 % 2, z2 * 4 + (y2 // 2) * 2 + core2

    def item_at(t):
        seq2, head2 = partner(t)
        shifted = (head2 >= H // 2).astype(jnp.int32)
        plane = (ctx + 4 - shifted * (1 - seq)) % 4
        return seq2, head2, plane, (me + 32 * shifted) % BLOCKS

    def owner_at(t):
        seq2, head2 = partner(t)
        shifted = shifted_me.astype(jnp.int32)
        plane = (ctx + shifted * (1 - seq2)) % 4
        return seq2, head2, plane, (seq2 * 32 + head2 + 32 * shifted) % BLOCKS

    inputs = (q_in, k_in, v_in, g_in)
    loads = [
        pltpu.make_async_copy(inputs[a].at[0], held.at[a], load_sem.at[a]) for a in range(4)
    ]
    for load in loads:
        load.start()

    barrier = pltpu.get_barrier_semaphore()

    def greet(t, _):
        seq2, head2, plane, _ = owner_at(t)
        pl.semaphore_signal(barrier, inc=1, device_id=(seq2, plane, head2), device_id_type=MESH)
        return _

    lax.fori_loop(1, BLOCKS, greet, 0)

    @pl.when(jnp.logical_not(local))
    def _():
        greet(0, 0)

    def by_head(a):
        loads[a].wait()
        x = held[a].reshape(ROWS, BLOCKS, D)
        sent[a] = jnp.swapaxes(x, 0, 1).reshape(T, D)

    def send_in(n):
        first, count = IN_GROUPS[n]
        slots = pl.ds(first, count)

        def copy(t, send_sem):
            seq2, head2, plane, place = item_at(t)
            return pltpu.make_async_remote_copy(
                src_ref=sent.at[slots, rows(seq2 * 32 + head2)],
                dst_ref=items.at[slots, rows(place)],
                send_sem=send_sem,
                recv_sem=in_recv.at[n],
                device_id=(seq2, plane, head2),
                device_id_type=MESH,
            )

        @pl.when(local)
        def _():
            place = (me + 32 * shifted_me.astype(jnp.int32)) % BLOCKS
            pltpu.make_async_copy(
                sent.at[slots, rows(me)], items.at[slots, rows(place)], in_recv.at[n]
            ).start()

        @pl.when(jnp.logical_not(local))
        def _():
            copy(0, own_send.at[n]).start()

        def step(t, _):
            copy(t, in_send.at[n]).start()
            return _

        lax.fori_loop(1, BLOCKS, step, 0)

    def send_out(n):
        first, count = OUT_GROUPS[n]
        slots = pl.ds(first, count)

        def copy(t, send_sem):
            seq2, head2, plane, place = owner_at(t)
            return pltpu.make_async_remote_copy(
                src_ref=made.at[slots, rows(place)],
                dst_ref=given.at[slots, rows(me)],
                send_sem=send_sem,
                recv_sem=out_recv.at[n],
                device_id=(seq2, plane, head2),
                device_id_type=MESH,
            )

        @pl.when(local)
        def _():
            place = (me + 32 * shifted_me.astype(jnp.int32)) % BLOCKS
            pltpu.make_async_copy(
                made.at[slots, rows(place)], given.at[slots, rows(me)], out_recv.at[n]
            ).start()

        @pl.when(jnp.logical_not(local))
        def _():
            copy(0, own_send.at[3 + n]).start()

        def step(t, _):
            copy(t, out_send.at[n]).start()
            return _

        lax.fori_loop(1, BLOCKS, step, 0)

    def arrived(buffer, groups, sems, n):
        first, count = groups[n]
        whole = buffer.at[pl.ds(first, count)]
        pltpu.make_async_copy(whole, whole, sems.at[n]).wait()

    def left(buffer, groups, sems, n, own):
        first, count = groups[n]
        most = buffer.at[pl.ds(first, count), pl.ds(0, T - ROWS)]
        pltpu.make_async_copy(most, most, sems.at[n]).wait()

        @pl.when(jnp.logical_not(local))
        def _():
            one = buffer.at[pl.ds(first, count), pl.ds(0, ROWS)]
            pltpu.make_async_copy(one, one, own_send.at[own]).wait()

    by_head(0)
    by_head(1)
    pl.semaphore_wait(barrier, BLOCKS - local.astype(jnp.int32))
    send_in(0)
    by_head(2)
    send_in(1)
    by_head(3)
    send_in(2)

    q, k, v, g = (items.at[a] for a in range(4))
    arrived(items, IN_GROUPS, in_recv, 0)
    softmax_weights(q, k, scores, weights)
    k_t[...] = k[...].T
    arrived(items, IN_GROUPS, in_recv, 1)
    v_t[...] = v[...].T
    attended(v_t, weights, made.at[0], out_wide)
    send_out(0)
    arrived(items, IN_GROUPS, in_recv, 2)
    value_grads(weights, g, made.at[1])
    send_out(1)
    row_dots(g, out_wide, row_dot)
    score_grads(weights, q, k_t, v, g, row_dot, ds, made.at[2], made.at[3])
    send_out(2)

    for n in range(3):
        left(sent, IN_GROUPS, in_send, n, n)

    outputs = (o_out, dv_out, dq_out, dk_out)
    stores = []
    for n, (first, count) in enumerate(OUT_GROUPS):
        arrived(given, OUT_GROUPS, out_recv, n)
        for a in range(first, first + count):
            x = given[a].reshape(BLOCKS, ROWS, D)
            held[a] = jnp.swapaxes(x, 0, 1).reshape(ROWS, 2, H, D)
            store = pltpu.make_async_copy(held.at[a], outputs[a].at[0], store_sem.at[a])
            store.start()
            stores.append(store)
    for n in range(3):
        left(made, OUT_GROUPS, out_send, n, 3 + n)
    for store in stores:
        store.wait()


def shards(queries, key_states, value_states, output_grad):
    any_space = pl.BlockSpec(memory_space=pl.ANY)
    block = jax.ShapeDtypeStruct(queries.shape, jnp.bfloat16)
    low, wide = jnp.bfloat16, jnp.float32
    results = pl.pallas_call(
        kernel,
        out_shape=[block] * 4,
        in_specs=[any_space] * 4,
        out_specs=[any_space] * 4,
        scratch_shapes=[
            pltpu.VMEM((4, ROWS, 2, H, D), low),
            pltpu.VMEM((4, T, D), low),
            pltpu.VMEM((4, T, D), low),
            pltpu.VMEM((4, T, D), low),
            pltpu.VMEM((4, T, D), low),
            pltpu.VMEM((T, TB), wide),
            pltpu.VMEM((T, T), low),
            pltpu.VMEM((T, T), low),
            pltpu.VMEM((D, T), low),
            pltpu.VMEM((D, T), low),
            pltpu.VMEM((T, D), wide),
            pltpu.VMEM((8, T), wide),
            pltpu.SemaphoreType.DMA((4,)),
            pltpu.SemaphoreType.DMA((4,)),
            pltpu.SemaphoreType.DMA((3,)),
            pltpu.SemaphoreType.DMA((3,)),
            pltpu.SemaphoreType.DMA((3,)),
            pltpu.SemaphoreType.DMA((3,)),
            pltpu.SemaphoreType.DMA((6,)),
        ],
        compiler_params=pltpu.CompilerParams(
            collective_id=0, has_side_effects=True, vmem_limit_bytes=56 << 20
        ),
        cost_estimate=pl.CostEstimate(
            flops=12 * T * T * D // 2, bytes_accessed=16 * T * D, transcendentals=T * T // 2
        ),
        name="shifted_attention",
    )(queries, key_states, value_states, output_grad)
    return tuple(results)


def solution(mesh):
    spec = P("ctx", ("seq", "head"), None, None, None)
    return jax.shard_map(
        shards, mesh=mesh, in_specs=(spec,) * 4, out_specs=(spec,) * 4, check_vma=False
    )
```

```python
import functools
import math

import jax
import jax.numpy as jnp
from jax import lax
from jax.experimental import pallas as pl
from jax.experimental.pallas import tpu as pltpu
from jax.sharding import PartitionSpec as P

H = 32
T = 2048
D = 128
BLOCKS = 64
ROWS = T // BLOCKS
TB = 256
NB = T // TB
SCALE = D**-0.5
EXP2_SCALE = SCALE * math.log2(math.e)
NT = (((1,), (1,)), ((), ()))
NN = (((1,), (0,)), ((), ()))
MESH = pl.DeviceIdType.MESH
IN_GROUPS = ((0, 2), (2, 1), (3, 1))
OUT_GROUPS = ((0, 1), (1, 1), (2, 2))


def dot(a, b, dims=NN):
    return lax.dot_general(a, b, dims, preferred_element_type=jnp.float32)


def tile(i, n=1):
    return pl.ds(i * TB, n * TB)


def rows(block):
    return pl.ds(pl.multiple_of(block * ROWS, ROWS), ROWS)


def softmax_weights(q, k, scores, weights):
    for i in range(NB):
        q_tile = q[tile(i)]
        top = None
        for j in range(i + 1):
            s = dot(k[tile(j)], q_tile, NT)
            if j == i:
                key_pos = lax.broadcasted_iota(jnp.int32, (TB, TB), 0)
                query_pos = lax.broadcasted_iota(jnp.int32, (TB, TB), 1)
                s = jnp.where(key_pos <= query_pos, s, -jnp.inf)
            scores[tile(j)] = s
            part = jnp.max(s, axis=0, keepdims=True)
            top = part if top is None else jnp.maximum(top, part)
        shift = top * EXP2_SCALE
        total = None
        for j in range(i + 1):
            e = jnp.exp2(scores[tile(j)] * EXP2_SCALE - shift)
            scores[tile(j)] = e
            part = jnp.sum(e, axis=0, keepdims=True)
            total = part if total is None else total + part
        inverse = 1.0 / total
        for j in range(i + 1):
            weights[tile(j), tile(i)] = (scores[tile(j)] * inverse).astype(jnp.bfloat16)


def attended(v_t, weights, out, out_wide):
    for i in range(NB):
        o = dot(v_t[:, 0 : (i + 1) * TB], weights[0 : (i + 1) * TB, tile(i)]).T
        out_wide[tile(i)] = o
        out[tile(i)] = o.astype(jnp.bfloat16)


def value_grads(weights, g, dv):
    for j in range(NB):
        n = NB - j
        dv[tile(j)] = dot(weights[tile(j), tile(j, n)], g[tile(j, n)]).astype(jnp.bfloat16)


def row_dots(g, out_wide, row_dot):
    ones = jnp.ones((8, D), jnp.bfloat16)
    for i in range(NB):
        x = g[tile(i)].astype(jnp.float32) * out_wide[tile(i)]
        high = x.astype(jnp.bfloat16)
        low = (x - high.astype(jnp.float32)).astype(jnp.bfloat16)
        row_dot[:, tile(i)] = dot(ones, high, NT) + dot(ones, low, NT)


def score_grads(weights, q, k_t, v, g, row_dot, ds, dq, dk):
    for i in range(NB):
        r = row_dot[0:1, tile(i)]
        for j in range(i + 1):
            dp = dot(v[tile(j)], g[tile(i)], NT)
            w = weights[tile(j), tile(i)].astype(jnp.float32)
            ds[tile(j), tile(i)] = (w * (dp - r)).astype(jnp.bfloat16)
        grad = dot(k_t[:, 0 : (i + 1) * TB], ds[0 : (i + 1) * TB, tile(i)])
        dq[tile(i)] = (grad * SCALE).T.astype(jnp.bfloat16)
    for j in range(NB):
        n = NB - j
        dk[tile(j)] = (dot(ds[tile(j), tile(j, n)], q[tile(j, n)]) * SCALE).astype(jnp.bfloat16)


def kernel(
    q_in, k_in, v_in, g_in, o_out, dq_out, dk_out, dv_out,
    held, sent, items, made, given,
    scores, weights, ds, v_t, k_t, out_wide, row_dot,
    load_sem, store_sem, in_send, in_recv, out_send, out_recv, own_send,
):
    seq = lax.axis_index("seq")
    ctx = lax.axis_index("ctx")
    head = lax.axis_index("head")
    me = seq * 32 + head
    z = head // 4
    y = ((head // 2) % 2) * 2 + seq
    core = head % 2
    shifted_me = head >= H // 2
    local = jnp.logical_or(jnp.logical_not(shifted_me), seq == 1)

    def partner(t):
        e = t // 8
        z2 = (z + 3 * t) % 8
        y2 = (y + e) % 4
        core2 = (core + e // 4) % 2
        return y2 % 2, z2 * 4 + (y2 // 2) * 2 + core2

    def item_at(t):
        seq2, head2 = partner(t)
        shifted = (head2 >= H // 2).astype(jnp.int32)
        plane = (ctx + 4 - shifted * (1 - seq)) % 4
        return seq2, head2, plane, (me + 32 * shifted) % BLOCKS

    def owner_at(t):
        seq2, head2 = partner(t)
        shifted = shifted_me.astype(jnp.int32)
        plane = (ctx + shifted * (1 - seq2)) % 4
        return seq2, head2, plane, (seq2 * 32 + head2 + 32 * shifted) % BLOCKS

    inputs = (q_in, k_in, v_in, g_in)
    loads = [
        pltpu.make_async_copy(inputs[a].at[0], held.at[a], load_sem.at[a]) for a in range(4)
    ]
    for load in loads:
        load.start()

    barrier = pltpu.get_barrier_semaphore()

    def greet(t, _):
        seq2, head2, plane, _ = owner_at(t)
        pl.semaphore_signal(barrier, inc=1, device_id=(seq2, plane, head2), device_id_type=MESH)
        return _

    lax.fori_loop(1, BLOCKS, greet, 0)

    @pl.when(jnp.logical_not(local))
    def _():
        greet(0, 0)

    def by_head(a):
        loads[a].wait()
        x = held[a].reshape(ROWS, BLOCKS, D)
        sent[a] = jnp.swapaxes(x, 0, 1).reshape(T, D)

    def send_in(n):
        first, count = IN_GROUPS[n]
        slots = pl.ds(first, count)

        def copy(t, send_sem):
            seq2, head2, plane, place = item_at(t)
            return pltpu.make_async_remote_copy(
                src_ref=sent.at[slots, rows(seq2 * 32 + head2)],
                dst_ref=items.at[slots, rows(place)],
                send_sem=send_sem,
                recv_sem=in_recv.at[n],
                device_id=(seq2, plane, head2),
                device_id_type=MESH,
            )

        @pl.when(local)
        def _():
            place = (me + 32 * shifted_me.astype(jnp.int32)) % BLOCKS
            pltpu.make_async_copy(
                sent.at[slots, rows(me)], items.at[slots, rows(place)], in_recv.at[n]
            ).start()

        @pl.when(jnp.logical_not(local))
        def _():
            copy(0, own_send.at[n]).start()

        def step(t, _):
            copy(t, in_send.at[n]).start()
            return _

        lax.fori_loop(1, BLOCKS, step, 0)

    def send_out(n):
        first, count = OUT_GROUPS[n]
        slots = pl.ds(first, count)

        def copy(t, send_sem):
            seq2, head2, plane, place = owner_at(t)
            return pltpu.make_async_remote_copy(
                src_ref=made.at[slots, rows(place)],
                dst_ref=given.at[slots, rows(me)],
                send_sem=send_sem,
                recv_sem=out_recv.at[n],
                device_id=(seq2, plane, head2),
                device_id_type=MESH,
            )

        @pl.when(local)
        def _():
            place = (me + 32 * shifted_me.astype(jnp.int32)) % BLOCKS
            pltpu.make_async_copy(
                made.at[slots, rows(place)], given.at[slots, rows(me)], out_recv.at[n]
            ).start()

        @pl.when(jnp.logical_not(local))
        def _():
            copy(0, own_send.at[3 + n]).start()

        def step(t, _):
            copy(t, out_send.at[n]).start()
            return _

        lax.fori_loop(1, BLOCKS, step, 0)

    def arrived(buffer, groups, sems, n):
        first, count = groups[n]
        whole = buffer.at[pl.ds(first, count)]
        pltpu.make_async_copy(whole, whole, sems.at[n]).wait()

    def left(buffer, groups, sems, n, own):
        first, count = groups[n]
        most = buffer.at[pl.ds(first, count), pl.ds(0, T - ROWS)]
        pltpu.make_async_copy(most, most, sems.at[n]).wait()

        @pl.when(jnp.logical_not(local))
        def _():
            one = buffer.at[pl.ds(first, count), pl.ds(0, ROWS)]
            pltpu.make_async_copy(one, one, own_send.at[own]).wait()

    by_head(0)
    by_head(1)
    pl.semaphore_wait(barrier, BLOCKS - local.astype(jnp.int32))
    send_in(0)
    by_head(2)
    send_in(1)
    by_head(3)
    send_in(2)

    q, k, v, g = (items.at[a] for a in range(4))
    arrived(items, IN_GROUPS, in_recv, 0)
    softmax_weights(q, k, scores, weights)
    k_t[...] = k[...].T
    arrived(items, IN_GROUPS, in_recv, 1)
    v_t[...] = v[...].T
    attended(v_t, weights, made.at[0], out_wide)
    send_out(0)
    arrived(items, IN_GROUPS, in_recv, 2)
    value_grads(weights, g, made.at[1])
    send_out(1)
    row_dots(g, out_wide, row_dot)
    score_grads(weights, q, k_t, v, g, row_dot, ds, made.at[2], made.at[3])
    send_out(2)

    for n in range(3):
        left(sent, IN_GROUPS, in_send, n, n)

    outputs = (o_out, dv_out, dq_out, dk_out)
    for n, (first, count) in enumerate(OUT_GROUPS):
        arrived(given, OUT_GROUPS, out_recv, n)
        for a in range(first, first + count):
            x = given[a].reshape(BLOCKS, ROWS, D)
            outputs[a][0] = jnp.swapaxes(x, 0, 1).reshape(ROWS, 2, H, D)
    for n in range(3):
        left(made, OUT_GROUPS, out_send, n, 3 + n)


def store_results(*refs):
    sems = refs[8]
    copies = [pltpu.make_async_copy(refs[a], refs[4 + a], sems.at[a]) for a in range(4)]
    for copy in copies:
        copy.start()
    for copy in copies:
        copy.wait()


def shards(queries, key_states, value_states, output_grad):
    in_vmem = pl.BlockSpec(memory_space=pltpu.VMEM)
    in_hbm = pl.BlockSpec(memory_space=pltpu.HBM)
    block = jax.ShapeDtypeStruct(queries.shape, jnp.bfloat16)
    low, wide = jnp.bfloat16, jnp.float32
    results = pl.pallas_call(
        kernel,
        out_shape=[pltpu.VMEM(queries.shape, low)] * 4,
        in_specs=[in_hbm] * 4,
        out_specs=[in_vmem] * 4,
        scratch_shapes=[
            pltpu.VMEM((4, ROWS, 2, H, D), low),
            pltpu.VMEM((4, T, D), low),
            pltpu.VMEM((4, T, D), low),
            pltpu.VMEM((4, T, D), low),
            pltpu.VMEM((4, T, D), low),
            pltpu.VMEM((T, TB), wide),
            pltpu.VMEM((T, T), low),
            pltpu.VMEM((T, T), low),
            pltpu.VMEM((D, T), low),
            pltpu.VMEM((D, T), low),
            pltpu.VMEM((T, D), wide),
            pltpu.VMEM((8, T), wide),
            pltpu.SemaphoreType.DMA((4,)),
            pltpu.SemaphoreType.DMA((4,)),
            pltpu.SemaphoreType.DMA((3,)),
            pltpu.SemaphoreType.DMA((3,)),
            pltpu.SemaphoreType.DMA((3,)),
            pltpu.SemaphoreType.DMA((3,)),
            pltpu.SemaphoreType.DMA((6,)),
        ],
        compiler_params=pltpu.CompilerParams(
            collective_id=0, has_side_effects=True, vmem_limit_bytes=36 << 20
        ),
        cost_estimate=pl.CostEstimate(
            flops=12 * T * T * D // 2, bytes_accessed=16 * T * D, transcendentals=T * T // 2
        ),
        name="shifted_attention",
    )(*[
        pltpu.with_memory_space_constraint(x, pltpu.HBM)
        for x in (queries, key_states, value_states, output_grad)
    ])
    return tuple(
        pl.pallas_call(
            store_results,
            out_shape=[block] * 4,
            in_specs=[in_vmem] * 4,
            out_specs=[in_hbm] * 4,
            scratch_shapes=[pltpu.SemaphoreType.DMA((4,))],
            compiler_params=pltpu.CompilerParams(vmem_limit_bytes=4 << 20),
            name="store_results",
        )(*[pltpu.with_memory_space_constraint(x, pltpu.VMEM) for x in results])
    )


def solution(mesh):
    spec = P("ctx", ("seq", "head"), None, None, None)
    return jax.shard_map(
        shards, mesh=mesh, in_specs=(spec,) * 4, out_specs=(spec,) * 4, check_vma=False
    )
```

```python
import functools
import math

import jax
import jax.numpy as jnp
from jax import lax
from jax.experimental import pallas as pl
from jax.experimental.pallas import tpu as pltpu
from jax.sharding import PartitionSpec as P

H = 32
T = 2048
D = 128
BLOCKS = 64
ROWS = T // BLOCKS
TB = 256
NB = T // TB
SCALE = D**-0.5
EXP2_SCALE = SCALE * math.log2(math.e)
NT = (((1,), (1,)), ((), ()))
NN = (((1,), (0,)), ((), ()))
MESH = pl.DeviceIdType.MESH
FAR_FIRST = ((4,), (3, 5), (2, 6), (1, 7))


def dot(a, b, dims=NN):
    return lax.dot_general(a, b, dims, preferred_element_type=jnp.float32)


def tile(i, n=1):
    return pl.ds(i * TB, n * TB)


def rows(block):
    return pl.ds(pl.multiple_of(block * ROWS, ROWS), ROWS)


def softmax_weights(q, k, scores, weights):
    for i in range(NB):
        q_tile = q[tile(i)]
        top = None
        for j in range(i + 1):
            s = dot(k[tile(j)], q_tile, NT)
            if j == i:
                key_pos = lax.broadcasted_iota(jnp.int32, (TB, TB), 0)
                query_pos = lax.broadcasted_iota(jnp.int32, (TB, TB), 1)
                s = jnp.where(key_pos <= query_pos, s, -jnp.inf)
            scores[tile(j)] = s
            part = jnp.max(s, axis=0, keepdims=True)
            top = part if top is None else jnp.maximum(top, part)
        shift = top * EXP2_SCALE
        total = None
        for j in range(i + 1):
            e = jnp.exp2(scores[tile(j)] * EXP2_SCALE - shift)
            scores[tile(j)] = e
            part = jnp.sum(e, axis=0, keepdims=True)
            total = part if total is None else total + part
        inverse = 1.0 / total
        for j in range(i + 1):
            weights[tile(j), tile(i)] = (scores[tile(j)] * inverse).astype(jnp.bfloat16)


def attended(v_t, weights, out, out_wide):
    for i in range(NB):
        o = dot(v_t[:, 0 : (i + 1) * TB], weights[0 : (i + 1) * TB, tile(i)]).T
        out_wide[tile(i)] = o
        out[tile(i)] = o.astype(jnp.bfloat16)


def value_grads(weights, g, dv):
    for j in range(NB):
        n = NB - j
        dv[tile(j)] = dot(weights[tile(j), tile(j, n)], g[tile(j, n)]).astype(jnp.bfloat16)


def row_dots(g, out_wide, row_dot):
    ones = jnp.ones((8, D), jnp.bfloat16)
    for i in range(NB):
        x = g[tile(i)].astype(jnp.float32) * out_wide[tile(i)]
        high = x.astype(jnp.bfloat16)
        low = (x - high.astype(jnp.float32)).astype(jnp.bfloat16)
        row_dot[:, tile(i)] = dot(ones, high, NT) + dot(ones, low, NT)


def score_grads(weights, k_t, v, g, row_dot, ds, dq):
    for i in range(NB):
        r = row_dot[0:1, tile(i)]
        for j in range(i + 1):
            dp = dot(v[tile(j)], g[tile(i)], NT)
            w = weights[tile(j), tile(i)].astype(jnp.float32)
            ds[tile(j), tile(i)] = (w * (dp - r)).astype(jnp.bfloat16)
        grad = dot(k_t[:, 0 : (i + 1) * TB], ds[0 : (i + 1) * TB, tile(i)])
        dq[tile(i)] = (grad * SCALE).T.astype(jnp.bfloat16)


def key_grads(ds, q, dk):
    for j in range(NB):
        n = NB - j
        dk[tile(j)] = (dot(ds[tile(j), tile(j, n)], q[tile(j, n)]) * SCALE).astype(jnp.bfloat16)


def kernel(
    q_in, k_in, v_in, g_in, o_out, dq_out, dk_out, dv_out,
    held, sent, items, made, given,
    scores, weights, ds, v_t, k_t, out_wide, row_dot,
    load_sem, in_send, in_recv, out_send, out_recv, own_send, ring_sem,
):
    seq = lax.axis_index("seq")
    ctx = lax.axis_index("ctx")
    head = lax.axis_index("head")
    me = seq * 32 + head
    z = head // 4
    high = (head // 2) % 2
    y = high * 2 + seq
    core = head % 2
    def device(seq2, plane, z2, high2, core2):
        return seq2, plane, z2 * 4 + high2 * 2 + core2


    def index_of(seq2, z2, high2, core2):
        return seq2 * H + core2 * (H // 2) + z2 * 2 + high2

    def neighbour(e):
        y2 = (y + e) % 4
        return y2 % 2, y2 // 2, (core + e // 4) % 2

    def each_partner(visit):
        for distances in FAR_FIRST:
            starts = [(z + dz) % 8 for dz in distances]

            def step(e, carry, starts=starts):
                seq2, high2, core2 = neighbour(e)
                for z2 in starts:
                    visit(seq2, z2, high2, core2)
                return carry

            lax.fori_loop(0, 8, step, 0)

        def near(e, carry):
            seq2, high2, core2 = neighbour(e)
            visit(seq2, z, high2, core2)
            return carry

        lax.fori_loop(1, 8, near, 0)

    def item_at(seq2, z2, high2, core2):
        return (ctx + 4 - core2 * (1 - seq)) % 4, (me + 32 * core2) % BLOCKS

    def owner_at(seq2, z2, high2, core2):
        block = seq2 * 32 + z2 * 4 + high2 * 2 + core2
        return (ctx + core * (1 - seq2)) % 4, (block + 32 * core) % BLOCKS

    mine = index_of(seq, z, high, core)
    local = core * (1 - seq) == 0
    here = (seq, z, high, core)

    inputs = (q_in, k_in, v_in, g_in)
    loads = [
        pltpu.make_async_copy(inputs[a].at[0], held.at[a], load_sem.at[a]) for a in range(4)
    ]
    for load in loads:
        load.start()

    barrier = pltpu.get_barrier_semaphore()
    ring = [device(seq, ctx, (z + dz) % 8, high, core) for dz in range(1, 8)]

    def greet(seq2, high2, core2):
        plane, _ = owner_at(seq2, z, high2, core2)
        pl.semaphore_signal(
            barrier, inc=1, device_id=device(seq2, plane, z, high2, core2), device_id_type=MESH
        )

    def greet_neighbour(e, carry):
        greet(*neighbour(e))
        return carry

    lax.fori_loop(1, 8, greet_neighbour, 0)

    @pl.when(jnp.logical_not(local))
    def _():
        greet(seq, high, core)

    for to in ring:
        pl.semaphore_signal(barrier, inc=1, device_id=to, device_id_type=MESH)

    def all_in():
        pl.semaphore_wait(barrier, 15 - local.astype(jnp.int32))
        for to in ring:
            pl.semaphore_signal(ring_sem, inc=1, device_id=to, device_id_type=MESH)
        pl.semaphore_wait(ring_sem, 7)

    def by_head(a):
        loads[a].wait()
        x = held[a].reshape(ROWS, BLOCKS, D)
        sent[a] = jnp.swapaxes(x, 0, 1).reshape(T, D)

    def send_in(n):
        def copy(at, send_sem):
            plane, place = item_at(*at)
            return pltpu.make_async_remote_copy(
                src_ref=sent.at[n, rows(index_of(*at))],
                dst_ref=items.at[n, rows(place)],
                send_sem=send_sem,
                recv_sem=in_recv.at[n],
                device_id=device(at[0], plane, *at[1:]),
                device_id_type=MESH,
            )

        each_partner(lambda *at: copy(at, in_send.at[n]).start())

        @pl.when(local)
        def _():
            _, place = item_at(*here)
            pltpu.make_async_copy(
                sent.at[n, rows(mine)], items.at[n, rows(place)], in_recv.at[n]
            ).start()

        @pl.when(jnp.logical_not(local))
        def _():
            copy(here, own_send.at[n]).start()

    def send_out(n):
        def copy(at, send_sem):
            plane, place = owner_at(*at)
            return pltpu.make_async_remote_copy(
                src_ref=made.at[n, rows(place)],
                dst_ref=given.at[n, rows(mine)],
                send_sem=send_sem,
                recv_sem=out_recv.at[n],
                device_id=device(at[0], plane, *at[1:]),
                device_id_type=MESH,
            )

        each_partner(lambda *at: copy(at, out_send.at[n]).start())

        @pl.when(local)
        def _():
            _, place = owner_at(*here)
            pltpu.make_async_copy(
                made.at[n, rows(place)], given.at[n, rows(mine)], out_recv.at[n]
            ).start()

        @pl.when(jnp.logical_not(local))
        def _():
            copy(here, own_send.at[4 + n]).start()

    def arrived(buffer, sems, n):
        pltpu.make_async_copy(buffer.at[n], buffer.at[n], sems.at[n]).wait()

    def left(buffer, sems, n, own):
        most = buffer.at[n, pl.ds(0, T - ROWS)]
        pltpu.make_async_copy(most, most, sems.at[n]).wait()

        @pl.when(jnp.logical_not(local))
        def _():
            one = buffer.at[n, pl.ds(0, ROWS)]
            pltpu.make_async_copy(one, one, own_send.at[own]).wait()

    for n in range(4):
        by_head(n)
        if n == 0:
            all_in()
        send_in(n)

    q, k, v, g = (items.at[a] for a in range(4))
    o, dv, dq, dk = (made.at[a] for a in range(4))
    arrived(items, in_recv, 0)
    arrived(items, in_recv, 1)
    softmax_weights(q, k, scores, weights)
    k_t[...] = k[...].T
    arrived(items, in_recv, 2)
    v_t[...] = v[...].T
    attended(v_t, weights, o, out_wide)
    send_out(0)
    arrived(items, in_recv, 3)
    value_grads(weights, g, dv)
    send_out(1)
    row_dots(g, out_wide, row_dot)
    score_grads(weights, k_t, v, g, row_dot, ds, dq)
    send_out(2)
    key_grads(ds, q, dk)
    send_out(3)

    for n in range(4):
        left(sent, in_send, n, n)

    outputs = (o_out, dv_out, dq_out, dk_out)
    for n in range(4):
        arrived(given, out_recv, n)
        x = given[n].reshape(BLOCKS, ROWS, D)
        outputs[n][0] = jnp.swapaxes(x, 0, 1).reshape(ROWS, 2, H, D)
    for n in range(4):
        left(made, out_send, n, 4 + n)


def store_results(*refs):
    sems = refs[8]
    copies = [pltpu.make_async_copy(refs[a], refs[4 + a], sems.at[a]) for a in range(4)]
    for copy in copies:
        copy.start()
    for copy in copies:
        copy.wait()


def shards(queries, key_states, value_states, output_grad):
    in_vmem = pl.BlockSpec(memory_space=pltpu.VMEM)
    in_hbm = pl.BlockSpec(memory_space=pltpu.HBM)
    block = jax.ShapeDtypeStruct(queries.shape, jnp.bfloat16)
    low, wide = jnp.bfloat16, jnp.float32
    results = pl.pallas_call(
        kernel,
        out_shape=[pltpu.VMEM(queries.shape, low)] * 4,
        in_specs=[in_hbm] * 4,
        out_specs=[in_vmem] * 4,
        scratch_shapes=[
            pltpu.VMEM((4, ROWS, 2, H, D), low),
            pltpu.VMEM((4, T, D), low),
            pltpu.VMEM((4, T, D), low),
            pltpu.VMEM((4, T, D), low),
            pltpu.VMEM((4, T, D), low),
            pltpu.VMEM((T, TB), wide),
            pltpu.VMEM((T, T), low),
            pltpu.VMEM((T, T), low),
            pltpu.VMEM((D, T), low),
            pltpu.VMEM((D, T), low),
            pltpu.VMEM((T, D), wide),
            pltpu.VMEM((8, T), wide),
            pltpu.SemaphoreType.DMA((4,)),
            pltpu.SemaphoreType.DMA((4,)),
            pltpu.SemaphoreType.DMA((4,)),
            pltpu.SemaphoreType.DMA((4,)),
            pltpu.SemaphoreType.DMA((4,)),
            pltpu.SemaphoreType.DMA((8,)),
            pltpu.SemaphoreType.REGULAR,
        ],
        compiler_params=pltpu.CompilerParams(
            collective_id=0, has_side_effects=True, vmem_limit_bytes=36 << 20
        ),
        cost_estimate=pl.CostEstimate(
            flops=12 * T * T * D // 2, bytes_accessed=16 * T * D, transcendentals=T * T // 2
        ),
        name="shifted_attention",
    )(*[
        pltpu.with_memory_space_constraint(x, pltpu.HBM)
        for x in (queries, key_states, value_states, output_grad)
    ])
    return tuple(
        pl.pallas_call(
            store_results,
            out_shape=[block] * 4,
            in_specs=[in_vmem] * 4,
            out_specs=[in_hbm] * 4,
            scratch_shapes=[pltpu.SemaphoreType.DMA((4,))],
            compiler_params=pltpu.CompilerParams(vmem_limit_bytes=4 << 20),
            name="store_results",
        )(*[pltpu.with_memory_space_constraint(x, pltpu.VMEM) for x in results])
    )


def solution(mesh):
    spec = P("ctx", ("seq", "head"), None, None, None)
    return jax.shard_map(
        shards, mesh=mesh, in_specs=(spec,) * 4, out_specs=(spec,) * 4, check_vma=False
    )
```

```python
import functools
import math

import jax
import jax.numpy as jnp
from jax import lax
from jax.experimental import pallas as pl
from jax.experimental.pallas import tpu as pltpu
from jax.sharding import PartitionSpec as P

H = 32
T = 2048
D = 128
BLOCKS = 64
ROWS = T // BLOCKS
TB = 256
NB = T // TB
SCALE = D**-0.5
EXP2_SCALE = SCALE * math.log2(math.e)
NT = (((1,), (1,)), ((), ()))
NN = (((1,), (0,)), ((), ()))
MESH = pl.DeviceIdType.MESH
DISTANCES = (4, 0, 3, 5, 2, 6, 1, 7)


def dot(a, b, dims=NN):
    return lax.dot_general(a, b, dims, preferred_element_type=jnp.float32)


def tile(i, n=1):
    return pl.ds(i * TB, n * TB)


def rows(block):
    return pl.ds(pl.multiple_of(block * ROWS, ROWS), ROWS)


def softmax_weights(q, k, scores, weights):
    for i in range(NB):
        q_tile = q[tile(i)]
        top = None
        for j in range(i + 1):
            s = dot(k[tile(j)], q_tile, NT)
            if j == i:
                key_pos = lax.broadcasted_iota(jnp.int32, (TB, TB), 0)
                query_pos = lax.broadcasted_iota(jnp.int32, (TB, TB), 1)
                s = jnp.where(key_pos <= query_pos, s, -jnp.inf)
            scores[tile(j)] = s
            part = jnp.max(s, axis=0, keepdims=True)
            top = part if top is None else jnp.maximum(top, part)
        shift = top * EXP2_SCALE
        total = None
        for j in range(i + 1):
            e = jnp.exp2(scores[tile(j)] * EXP2_SCALE - shift)
            scores[tile(j)] = e
            part = jnp.sum(e, axis=0, keepdims=True)
            total = part if total is None else total + part
        inverse = 1.0 / total
        for j in range(i + 1):
            weights[tile(j), tile(i)] = (scores[tile(j)] * inverse).astype(jnp.bfloat16)


def attended(v_t, weights, out, out_wide):
    for i in range(NB):
        o = dot(v_t[:, 0 : (i + 1) * TB], weights[0 : (i + 1) * TB, tile(i)]).T
        out_wide[tile(i)] = o
        out[tile(i)] = o.astype(jnp.bfloat16)


def value_grads(weights, g, dv):
    for j in range(NB):
        n = NB - j
        dv[tile(j)] = dot(weights[tile(j), tile(j, n)], g[tile(j, n)]).astype(jnp.bfloat16)


def row_dots(g, out_wide, row_dot):
    ones = jnp.ones((8, D), jnp.bfloat16)
    for i in range(NB):
        x = g[tile(i)].astype(jnp.float32) * out_wide[tile(i)]
        high = x.astype(jnp.bfloat16)
        low = (x - high.astype(jnp.float32)).astype(jnp.bfloat16)
        row_dot[:, tile(i)] = dot(ones, high, NT) + dot(ones, low, NT)


def score_grads(weights, k_t, v, g, row_dot, ds, dq):
    for i in range(NB):
        r = row_dot[0:1, tile(i)]
        for j in range(i + 1):
            dp = dot(v[tile(j)], g[tile(i)], NT)
            w = weights[tile(j), tile(i)].astype(jnp.float32)
            ds[tile(j), tile(i)] = (w * (dp - r)).astype(jnp.bfloat16)
        grad = dot(k_t[:, 0 : (i + 1) * TB], ds[0 : (i + 1) * TB, tile(i)])
        dq[tile(i)] = (grad * SCALE).T.astype(jnp.bfloat16)


def key_grads(ds, q, dk):
    for j in range(NB):
        n = NB - j
        dk[tile(j)] = (dot(ds[tile(j), tile(j, n)], q[tile(j, n)]) * SCALE).astype(jnp.bfloat16)


def kernel(
    q_in, k_in, v_in, g_in, o_out, dq_out, dk_out, dv_out,
    held, sent, items, made, given,
    scores, weights, ds, v_t, k_t, out_wide, row_dot,
    load_sem, in_send, in_recv, out_send, out_recv, own_send,
):
    seq = lax.axis_index("seq")
    ctx = lax.axis_index("ctx")
    head = lax.axis_index("head")
    me = seq * 32 + head
    z = head // 4
    high = (head // 2) % 2
    y = high * 2 + seq
    core = head % 2

    def device(seq2, plane, z2, high2, core2):
        return seq2, plane, z2 * 4 + high2 * 2 + core2


    def index_of(seq2, z2, high2, core2):
        return seq2 * H + core2 * (H // 2) + z2 * 2 + high2

    def neighbour(e):
        y2 = (y + e) % 4
        return y2 % 2, y2 // 2, (core + e // 4) % 2

    def each_partner(visit):
        starts = [(z + dz) % 8 for dz in DISTANCES]
        for dz, z2 in zip(DISTANCES, starts):
            if dz:
                visit(seq, z2, high, core)

        def step(e, carry):
            seq2, high2, core2 = neighbour(e)
            for z2 in starts:
                visit(seq2, z2, high2, core2)
            return carry

        lax.fori_loop(1, 8, step, 0)

    def item_at(seq2, z2, high2, core2):
        return (ctx + 4 - core2 * (1 - seq)) % 4, (me + 32 * core2) % BLOCKS

    def owner_at(seq2, z2, high2, core2):
        block = seq2 * 32 + z2 * 4 + high2 * 2 + core2
        return (ctx + core * (1 - seq2)) % 4, (block + 32 * core) % BLOCKS

    mine = index_of(seq, z, high, core)
    local = core * (1 - seq) == 0
    here = (seq, z, high, core)

    barrier = pltpu.get_barrier_semaphore()

    def greet(*at):
        plane, _ = owner_at(*at)
        pl.semaphore_signal(
            barrier, inc=1, device_id=device(at[0], plane, *at[1:]), device_id_type=MESH
        )

    for e in range(8):
        seq2, high2, core2 = neighbour(e)
        for dz in DISTANCES:
            if (e, dz) != (0, 0):
                greet(seq2, (z + dz) % 8, high2, core2)

    @pl.when(jnp.logical_not(local))
    def _():
        greet(*here)

    inputs = (q_in, k_in, v_in, g_in)
    loads = [
        pltpu.make_async_copy(inputs[a].at[0], held.at[a], load_sem.at[a]) for a in range(4)
    ]
    for load in loads:
        load.start()

    def by_head(a):
        loads[a].wait()
        x = held[a].reshape(ROWS, BLOCKS, D)
        sent[a] = jnp.swapaxes(x, 0, 1).reshape(T, D)

    def send_in(n):
        def copy(at, send_sem):
            plane, place = item_at(*at)
            return pltpu.make_async_remote_copy(
                src_ref=sent.at[n, rows(index_of(*at))],
                dst_ref=items.at[n, rows(place)],
                send_sem=send_sem,
                recv_sem=in_recv.at[n],
                device_id=device(at[0], plane, *at[1:]),
                device_id_type=MESH,
            )

        each_partner(lambda *at: copy(at, in_send.at[n]).start())

        @pl.when(local)
        def _():
            _, place = item_at(*here)
            pltpu.make_async_copy(
                sent.at[n, rows(mine)], items.at[n, rows(place)], in_recv.at[n]
            ).start()

        @pl.when(jnp.logical_not(local))
        def _():
            copy(here, own_send.at[n]).start()

    def send_out(n):
        def copy(at, send_sem):
            plane, place = owner_at(*at)
            return pltpu.make_async_remote_copy(
                src_ref=made.at[n, rows(place)],
                dst_ref=given.at[n, rows(mine)],
                send_sem=send_sem,
                recv_sem=out_recv.at[n],
                device_id=device(at[0], plane, *at[1:]),
                device_id_type=MESH,
            )

        each_partner(lambda *at: copy(at, out_send.at[n]).start())

        @pl.when(local)
        def _():
            _, place = owner_at(*here)
            pltpu.make_async_copy(
                made.at[n, rows(place)], given.at[n, rows(mine)], out_recv.at[n]
            ).start()

        @pl.when(jnp.logical_not(local))
        def _():
            copy(here, own_send.at[4 + n]).start()

    def arrived(buffer, sems, n):
        pltpu.make_async_copy(buffer.at[n], buffer.at[n], sems.at[n]).wait()

    def left(buffer, sems, n, own):
        most = buffer.at[n, pl.ds(0, T - ROWS)]
        pltpu.make_async_copy(most, most, sems.at[n]).wait()

        @pl.when(jnp.logical_not(local))
        def _():
            one = buffer.at[n, pl.ds(0, ROWS)]
            pltpu.make_async_copy(one, one, own_send.at[own]).wait()

    for n in range(4):
        by_head(n)
        if n == 0:
            pl.semaphore_wait(barrier, BLOCKS - local.astype(jnp.int32))
        send_in(n)

    q, k, v, g = (items.at[a] for a in range(4))
    o, dv, dq, dk = (made.at[a] for a in range(4))
    arrived(items, in_recv, 0)
    arrived(items, in_recv, 1)
    softmax_weights(q, k, scores, weights)
    k_t[...] = k[...].T
    arrived(items, in_recv, 2)
    v_t[...] = v[...].T
    attended(v_t, weights, o, out_wide)
    send_out(0)
    arrived(items, in_recv, 3)
    value_grads(weights, g, dv)
    send_out(1)
    row_dots(g, out_wide, row_dot)
    score_grads(weights, k_t, v, g, row_dot, ds, dq)
    send_out(2)
    key_grads(ds, q, dk)
    send_out(3)

    for n in range(4):
        left(sent, in_send, n, n)

    outputs = (o_out, dv_out, dq_out, dk_out)
    for n in range(4):
        arrived(given, out_recv, n)
        x = given[n].reshape(BLOCKS, ROWS, D)
        outputs[n][0] = jnp.swapaxes(x, 0, 1).reshape(ROWS, 2, H, D)
    for n in range(4):
        left(made, out_send, n, 4 + n)


def store_results(*refs):
    sems = refs[8]
    copies = [pltpu.make_async_copy(refs[a], refs[4 + a], sems.at[a]) for a in range(4)]
    for copy in copies:
        copy.start()
    for copy in copies:
        copy.wait()


def shards(queries, key_states, value_states, output_grad):
    in_vmem = pl.BlockSpec(memory_space=pltpu.VMEM)
    in_hbm = pl.BlockSpec(memory_space=pltpu.HBM)
    block = jax.ShapeDtypeStruct(queries.shape, jnp.bfloat16)
    low, wide = jnp.bfloat16, jnp.float32
    results = pl.pallas_call(
        kernel,
        out_shape=[pltpu.VMEM(queries.shape, low)] * 4,
        in_specs=[in_hbm] * 4,
        out_specs=[in_vmem] * 4,
        scratch_shapes=[
            pltpu.VMEM((4, ROWS, 2, H, D), low),
            pltpu.VMEM((4, T, D), low),
            pltpu.VMEM((4, T, D), low),
            pltpu.VMEM((4, T, D), low),
            pltpu.VMEM((4, T, D), low),
            pltpu.VMEM((T, TB), wide),
            pltpu.VMEM((T, T), low),
            pltpu.VMEM((T, T), low),
            pltpu.VMEM((D, T), low),
            pltpu.VMEM((D, T), low),
            pltpu.VMEM((T, D), wide),
            pltpu.VMEM((8, T), wide),
            pltpu.SemaphoreType.DMA((4,)),
            pltpu.SemaphoreType.DMA((4,)),
            pltpu.SemaphoreType.DMA((4,)),
            pltpu.SemaphoreType.DMA((4,)),
            pltpu.SemaphoreType.DMA((4,)),
            pltpu.SemaphoreType.DMA((8,)),
        ],
        compiler_params=pltpu.CompilerParams(
            collective_id=0, has_side_effects=True, vmem_limit_bytes=36 << 20
        ),
        cost_estimate=pl.CostEstimate(
            flops=12 * T * T * D // 2, bytes_accessed=16 * T * D, transcendentals=T * T // 2
        ),
        name="shifted_attention",
    )(*[
        pltpu.with_memory_space_constraint(x, pltpu.HBM)
        for x in (queries, key_states, value_states, output_grad)
    ])
    return tuple(
        pl.pallas_call(
            store_results,
            out_shape=[block] * 4,
            in_specs=[in_vmem] * 4,
            out_specs=[in_hbm] * 4,
            scratch_shapes=[pltpu.SemaphoreType.DMA((4,))],
            compiler_params=pltpu.CompilerParams(vmem_limit_bytes=4 << 20),
            name="store_results",
        )(*[pltpu.with_memory_space_constraint(x, pltpu.VMEM) for x in results])
    )


def solution(mesh):
    spec = P("ctx", ("seq", "head"), None, None, None)
    return jax.shard_map(
        shards, mesh=mesh, in_specs=(spec,) * 4, out_specs=(spec,) * 4, check_vma=False
    )
```

```python
import functools
import math

import jax
import jax.numpy as jnp
from jax import lax
from jax.experimental import pallas as pl
from jax.experimental.pallas import tpu as pltpu
from jax.sharding import PartitionSpec as P

H = 32
T = 2048
D = 128
BLOCKS = 64
ROWS = T // BLOCKS
TB = 256
NB = T // TB
SCALE = D**-0.5
EXP2_SCALE = SCALE * math.log2(math.e)
NT = (((1,), (1,)), ((), ()))
NN = (((1,), (0,)), ((), ()))
MESH = pl.DeviceIdType.MESH
DISTANCES = (4, 0, 3, 5, 2, 6, 1, 7)


def dot(a, b, dims=NN):
    return lax.dot_general(a, b, dims, preferred_element_type=jnp.float32)


def tile(i, n=1):
    return pl.ds(i * TB, n * TB)


def rows(block):
    return pl.ds(pl.multiple_of(block * ROWS, ROWS), ROWS)


def softmax_weights(q, k, scores, weights):
    for i in range(NB):
        q_tile = q[tile(i)]
        top = None
        for j in range(i + 1):
            s = dot(k[tile(j)], q_tile, NT)
            if j == i:
                key_pos = lax.broadcasted_iota(jnp.int32, (TB, TB), 0)
                query_pos = lax.broadcasted_iota(jnp.int32, (TB, TB), 1)
                s = jnp.where(key_pos <= query_pos, s, -jnp.inf)
            scores[tile(j)] = s
            part = jnp.max(s, axis=0, keepdims=True)
            top = part if top is None else jnp.maximum(top, part)
        shift = top * EXP2_SCALE
        total = None
        for j in range(i + 1):
            e = jnp.exp2(scores[tile(j)] * EXP2_SCALE - shift)
            scores[tile(j)] = e
            part = jnp.sum(e, axis=0, keepdims=True)
            total = part if total is None else total + part
        inverse = 1.0 / total
        for j in range(i + 1):
            weights[tile(j), tile(i)] = (scores[tile(j)] * inverse).astype(jnp.bfloat16)


def attended(v_t, weights, out, out_wide):
    for i in range(NB):
        o = dot(v_t[:, 0 : (i + 1) * TB], weights[0 : (i + 1) * TB, tile(i)]).T
        out_wide[tile(i)] = o
        out[tile(i)] = o.astype(jnp.bfloat16)


def value_grads(weights, g, dv):
    for j in range(NB):
        n = NB - j
        dv[tile(j)] = dot(weights[tile(j), tile(j, n)], g[tile(j, n)]).astype(jnp.bfloat16)


def row_dots(g, out_wide, row_dot):
    ones = jnp.ones((8, D), jnp.bfloat16)
    for i in range(NB):
        x = g[tile(i)].astype(jnp.float32) * out_wide[tile(i)]
        high = x.astype(jnp.bfloat16)
        low = (x - high.astype(jnp.float32)).astype(jnp.bfloat16)
        row_dot[:, tile(i)] = dot(ones, high, NT) + dot(ones, low, NT)


def score_grads(weights, k_t, v, g, row_dot, ds, dq):
    for i in range(NB):
        r = row_dot[0:1, tile(i)]
        for j in range(i + 1):
            dp = dot(v[tile(j)], g[tile(i)], NT)
            w = weights[tile(j), tile(i)].astype(jnp.float32)
            ds[tile(j), tile(i)] = (w * (dp - r)).astype(jnp.bfloat16)
        grad = dot(k_t[:, 0 : (i + 1) * TB], ds[0 : (i + 1) * TB, tile(i)])
        dq[tile(i)] = (grad * SCALE).T.astype(jnp.bfloat16)


def key_grads(ds, q, dk):
    for j in range(NB):
        n = NB - j
        dk[tile(j)] = (dot(ds[tile(j), tile(j, n)], q[tile(j, n)]) * SCALE).astype(jnp.bfloat16)


def kernel(
    q_in, k_in, v_in, g_in, o_out, dq_out, dk_out, dv_out,
    held, sent, items, made, given,
    scores, weights, ds, v_t, k_t, out_wide, row_dot,
    load_sem, in_send, in_recv, out_send, out_recv, own_send,
):
    seq = lax.axis_index("seq")
    ctx = lax.axis_index("ctx")
    head = lax.axis_index("head")
    me = seq * 32 + head
    z = head // 4
    high = (head // 2) % 2
    y = high * 2 + seq
    core = head % 2

    def device(seq2, plane, z2, high2, core2):
        return seq2, plane, z2 * 4 + high2 * 2 + core2


    def index_of(seq2, z2, high2, core2):
        return seq2 * H + core2 * (H // 2) + z2 * 2 + high2

    def neighbour(e):
        y2 = (y + e + 1) % 4
        return y2 % 2, y2 // 2, (core + 1 + e // 4) % 2

    def each_partner(visit):
        starts = [(z + dz) % 8 for dz in DISTANCES]

        def step(e, carry):
            seq2, high2, core2 = neighbour(e)
            for z2 in starts:
                visit(seq2, z2, high2, core2)
            return carry

        lax.fori_loop(0, 7, step, 0)
        for dz, z2 in zip(DISTANCES, starts):
            if dz:
                visit(seq, z2, high, core)

    def item_at(seq2, z2, high2, core2):
        return (ctx + 4 - core2 * (1 - seq)) % 4, (me + 32 * core2) % BLOCKS

    def owner_at(seq2, z2, high2, core2):
        block = seq2 * 32 + z2 * 4 + high2 * 2 + core2
        return (ctx + core * (1 - seq2)) % 4, (block + 32 * core) % BLOCKS

    mine = index_of(seq, z, high, core)
    local = core * (1 - seq) == 0
    here = (seq, z, high, core)

    barrier = pltpu.get_barrier_semaphore()

    def greet(*at):
        plane, _ = owner_at(*at)
        pl.semaphore_signal(
            barrier, inc=1, device_id=device(at[0], plane, *at[1:]), device_id_type=MESH
        )

    for e in range(8):
        seq2, high2, core2 = neighbour(e)
        for dz in DISTANCES:
            if (e, dz) != (7, 0):
                greet(seq2, (z + dz) % 8, high2, core2)

    @pl.when(jnp.logical_not(local))
    def _():
        greet(*here)

    inputs = (q_in, k_in, v_in, g_in)
    loads = [
        pltpu.make_async_copy(inputs[a].at[0], held.at[a], load_sem.at[a]) for a in range(4)
    ]
    for load in loads:
        load.start()

    def by_head(a):
        loads[a].wait()
        x = held[a].reshape(ROWS, BLOCKS, D)
        sent[a] = jnp.swapaxes(x, 0, 1).reshape(T, D)

    def send_in(n):
        def copy(at, send_sem):
            plane, place = item_at(*at)
            return pltpu.make_async_remote_copy(
                src_ref=sent.at[n, rows(index_of(*at))],
                dst_ref=items.at[n, rows(place)],
                send_sem=send_sem,
                recv_sem=in_recv.at[n],
                device_id=device(at[0], plane, *at[1:]),
                device_id_type=MESH,
            )

        each_partner(lambda *at: copy(at, in_send.at[n]).start())

        @pl.when(local)
        def _():
            _, place = item_at(*here)
            pltpu.make_async_copy(
                sent.at[n, rows(mine)], items.at[n, rows(place)], in_recv.at[n]
            ).start()

        @pl.when(jnp.logical_not(local))
        def _():
            copy(here, own_send.at[n]).start()

    def send_out(n):
        def copy(at, send_sem):
            plane, place = owner_at(*at)
            return pltpu.make_async_remote_copy(
                src_ref=made.at[n, rows(place)],
                dst_ref=given.at[n, rows(mine)],
                send_sem=send_sem,
                recv_sem=out_recv.at[n],
                device_id=device(at[0], plane, *at[1:]),
                device_id_type=MESH,
            )

        each_partner(lambda *at: copy(at, out_send.at[n]).start())

        @pl.when(local)
        def _():
            _, place = owner_at(*here)
            pltpu.make_async_copy(
                made.at[n, rows(place)], given.at[n, rows(mine)], out_recv.at[n]
            ).start()

        @pl.when(jnp.logical_not(local))
        def _():
            copy(here, own_send.at[4 + n]).start()

    def arrived(buffer, sems, n):
        pltpu.make_async_copy(buffer.at[n], buffer.at[n], sems.at[n]).wait()

    def left(buffer, sems, n, own):
        most = buffer.at[n, pl.ds(0, T - ROWS)]
        pltpu.make_async_copy(most, most, sems.at[n]).wait()

        @pl.when(jnp.logical_not(local))
        def _():
            one = buffer.at[n, pl.ds(0, ROWS)]
            pltpu.make_async_copy(one, one, own_send.at[own]).wait()

    for n in range(4):
        by_head(n)
        if n == 0:
            pl.semaphore_wait(barrier, BLOCKS - local.astype(jnp.int32))
        send_in(n)

    q, k, v, g = (items.at[a] for a in range(4))
    o, dv, dq, dk = (made.at[a] for a in range(4))
    arrived(items, in_recv, 0)
    arrived(items, in_recv, 1)
    softmax_weights(q, k, scores, weights)
    k_t[...] = k[...].T
    arrived(items, in_recv, 2)
    v_t[...] = v[...].T
    attended(v_t, weights, o, out_wide)
    send_out(0)
    arrived(items, in_recv, 3)
    value_grads(weights, g, dv)
    send_out(1)
    row_dots(g, out_wide, row_dot)
    score_grads(weights, k_t, v, g, row_dot, ds, dq)
    send_out(2)
    key_grads(ds, q, dk)
    send_out(3)

    for n in range(4):
        left(sent, in_send, n, n)

    outputs = (o_out, dv_out, dq_out, dk_out)
    for n in range(4):
        arrived(given, out_recv, n)
        x = given[n].reshape(BLOCKS, ROWS, D)
        outputs[n][0] = jnp.swapaxes(x, 0, 1).reshape(ROWS, 2, H, D)
    for n in range(4):
        left(made, out_send, n, 4 + n)


def store_results(*refs):
    sems = refs[8]
    copies = [pltpu.make_async_copy(refs[a], refs[4 + a], sems.at[a]) for a in range(4)]
    for copy in copies:
        copy.start()
    for copy in copies:
        copy.wait()


def shards(queries, key_states, value_states, output_grad):
    in_vmem = pl.BlockSpec(memory_space=pltpu.VMEM)
    in_hbm = pl.BlockSpec(memory_space=pltpu.HBM)
    block = jax.ShapeDtypeStruct(queries.shape, jnp.bfloat16)
    low, wide = jnp.bfloat16, jnp.float32
    results = pl.pallas_call(
        kernel,
        out_shape=[pltpu.VMEM(queries.shape, low)] * 4,
        in_specs=[in_hbm] * 4,
        out_specs=[in_vmem] * 4,
        scratch_shapes=[
            pltpu.VMEM((4, ROWS, 2, H, D), low),
            pltpu.VMEM((4, T, D), low),
            pltpu.VMEM((4, T, D), low),
            pltpu.VMEM((4, T, D), low),
            pltpu.VMEM((4, T, D), low),
            pltpu.VMEM((T, TB), wide),
            pltpu.VMEM((T, T), low),
            pltpu.VMEM((T, T), low),
            pltpu.VMEM((D, T), low),
            pltpu.VMEM((D, T), low),
            pltpu.VMEM((T, D), wide),
            pltpu.VMEM((8, T), wide),
            pltpu.SemaphoreType.DMA((4,)),
            pltpu.SemaphoreType.DMA((4,)),
            pltpu.SemaphoreType.DMA((4,)),
            pltpu.SemaphoreType.DMA((4,)),
            pltpu.SemaphoreType.DMA((4,)),
            pltpu.SemaphoreType.DMA((8,)),
        ],
        compiler_params=pltpu.CompilerParams(
            collective_id=0, has_side_effects=True, vmem_limit_bytes=36 << 20
        ),
        cost_estimate=pl.CostEstimate(
            flops=12 * T * T * D // 2, bytes_accessed=16 * T * D, transcendentals=T * T // 2
        ),
        name="shifted_attention",
    )(*[
        pltpu.with_memory_space_constraint(x, pltpu.HBM)
        for x in (queries, key_states, value_states, output_grad)
    ])
    return tuple(
        pl.pallas_call(
            store_results,
            out_shape=[block] * 4,
            in_specs=[in_vmem] * 4,
            out_specs=[in_hbm] * 4,
            scratch_shapes=[pltpu.SemaphoreType.DMA((4,))],
            compiler_params=pltpu.CompilerParams(vmem_limit_bytes=4 << 20),
            name="store_results",
        )(*[pltpu.with_memory_space_constraint(x, pltpu.VMEM) for x in results])
    )


def solution(mesh):
    spec = P("ctx", ("seq", "head"), None, None, None)
    return jax.shard_map(
        shards, mesh=mesh, in_specs=(spec,) * 4, out_specs=(spec,) * 4, check_vma=False
    )
```

```python
import functools
import math

import jax
import jax.numpy as jnp
from jax import lax
from jax.experimental import pallas as pl
from jax.experimental.pallas import tpu as pltpu
from jax.sharding import PartitionSpec as P

H = 32
T = 2048
D = 128
BLOCKS = 64
ROWS = T // BLOCKS
TB = 256
NB = T // TB
SCALE = D**-0.5
EXP2_SCALE = SCALE * math.log2(math.e)
NT = (((1,), (1,)), ((), ()))
NN = (((1,), (0,)), ((), ()))
MESH = pl.DeviceIdType.MESH
DISTANCES = (4, 0, 3, 5, 2, 6, 1, 7)


FAR_TO_NEAR = sorted(
    ((e, dz) for e in range(8) for dz in DISTANCES if (e, dz) != (7, 0)),
    key=lambda at: -min(at[1], 8 - at[1]) - (1, 2, 1, 0)[at[0] % 4],
)


def dot(a, b, dims=NN):
    return lax.dot_general(a, b, dims, preferred_element_type=jnp.float32)


def tile(i, n=1):
    return pl.ds(i * TB, n * TB)


def rows(block):
    return pl.ds(pl.multiple_of(block * ROWS, ROWS), ROWS)


def softmax_weights(q, k, scores, weights):
    for i in range(NB):
        q_tile = q[tile(i)]
        top = None
        for j in range(i + 1):
            s = dot(k[tile(j)], q_tile, NT)
            if j == i:
                key_pos = lax.broadcasted_iota(jnp.int32, (TB, TB), 0)
                query_pos = lax.broadcasted_iota(jnp.int32, (TB, TB), 1)
                s = jnp.where(key_pos <= query_pos, s, -jnp.inf)
            scores[tile(j)] = s
            part = jnp.max(s, axis=0, keepdims=True)
            top = part if top is None else jnp.maximum(top, part)
        shift = top * EXP2_SCALE
        total = None
        for j in range(i + 1):
            e = jnp.exp2(scores[tile(j)] * EXP2_SCALE - shift)
            scores[tile(j)] = e
            part = jnp.sum(e, axis=0, keepdims=True)
            total = part if total is None else total + part
        inverse = 1.0 / total
        for j in range(i + 1):
            weights[tile(j), tile(i)] = (scores[tile(j)] * inverse).astype(jnp.bfloat16)


def attended(v_t, weights, out, out_wide):
    for i in range(NB):
        o = dot(v_t[:, 0 : (i + 1) * TB], weights[0 : (i + 1) * TB, tile(i)]).T
        out_wide[tile(i)] = o
        out[tile(i)] = o.astype(jnp.bfloat16)


def value_grads(weights, g, dv):
    for j in range(NB):
        n = NB - j
        dv[tile(j)] = dot(weights[tile(j), tile(j, n)], g[tile(j, n)]).astype(jnp.bfloat16)


def row_dots(g, out_wide, row_dot):
    ones = jnp.ones((8, D), jnp.bfloat16)
    for i in range(NB):
        x = g[tile(i)].astype(jnp.float32) * out_wide[tile(i)]
        high = x.astype(jnp.bfloat16)
        low = (x - high.astype(jnp.float32)).astype(jnp.bfloat16)
        row_dot[:, tile(i)] = dot(ones, high, NT) + dot(ones, low, NT)


def score_grads(weights, k_t, v, g, row_dot, ds, dq):
    for i in range(NB):
        r = row_dot[0:1, tile(i)]
        for j in range(i + 1):
            dp = dot(v[tile(j)], g[tile(i)], NT)
            w = weights[tile(j), tile(i)].astype(jnp.float32)
            ds[tile(j), tile(i)] = (w * (dp - r)).astype(jnp.bfloat16)
        grad = dot(k_t[:, 0 : (i + 1) * TB], ds[0 : (i + 1) * TB, tile(i)])
        dq[tile(i)] = (grad * SCALE).T.astype(jnp.bfloat16)


def key_grads(ds, q, dk):
    for j in range(NB):
        n = NB - j
        dk[tile(j)] = (dot(ds[tile(j), tile(j, n)], q[tile(j, n)]) * SCALE).astype(jnp.bfloat16)


def kernel(
    q_in, k_in, v_in, g_in, o_out, dq_out, dk_out, dv_out,
    held, sent, items, made, given,
    scores, weights, ds, v_t, k_t, out_wide, row_dot,
    load_sem, in_send, in_recv, out_send, out_recv, own_send,
):
    seq = lax.axis_index("seq")
    ctx = lax.axis_index("ctx")
    head = lax.axis_index("head")
    me = seq * 32 + head
    z = head // 4
    high = (head // 2) % 2
    y = high * 2 + seq
    core = head % 2

    def device(seq2, plane, z2, high2, core2):
        return seq2, plane, z2 * 4 + high2 * 2 + core2


    def index_of(seq2, z2, high2, core2):
        return seq2 * H + core2 * (H // 2) + z2 * 2 + high2

    def neighbour(e):
        y2 = (y + e + 1) % 4
        return y2 % 2, y2 // 2, (core + 1 + e // 4) % 2

    def each_partner(visit):
        starts = [(z + dz) % 8 for dz in DISTANCES]

        def step(e, carry):
            seq2, high2, core2 = neighbour(e)
            for z2 in starts:
                visit(seq2, z2, high2, core2)
            return carry

        lax.fori_loop(0, 7, step, 0)
        for dz, z2 in zip(DISTANCES, starts):
            if dz:
                visit(seq, z2, high, core)

    def item_at(seq2, z2, high2, core2):
        return (ctx + 4 - core2 * (1 - seq)) % 4, (me + 32 * core2) % BLOCKS

    def owner_at(seq2, z2, high2, core2):
        block = seq2 * 32 + z2 * 4 + high2 * 2 + core2
        return (ctx + core * (1 - seq2)) % 4, (block + 32 * core) % BLOCKS

    mine = index_of(seq, z, high, core)
    local = core * (1 - seq) == 0
    here = (seq, z, high, core)

    barrier = pltpu.get_barrier_semaphore()

    def greet(*at):
        plane, _ = owner_at(*at)
        pl.semaphore_signal(
            barrier, inc=1, device_id=device(at[0], plane, *at[1:]), device_id_type=MESH
        )

    for e, dz in FAR_TO_NEAR:
        seq2, high2, core2 = neighbour(e)
        greet(seq2, (z + dz) % 8, high2, core2)

    @pl.when(jnp.logical_not(local))
    def _():
        greet(*here)

    inputs = (q_in, k_in, v_in, g_in)
    loads = [
        pltpu.make_async_copy(inputs[a].at[0], held.at[a], load_sem.at[a]) for a in range(4)
    ]
    for load in loads:
        load.start()

    def by_head(a):
        loads[a].wait()
        x = held[a].reshape(ROWS, BLOCKS, D)
        sent[a] = jnp.swapaxes(x, 0, 1).reshape(T, D)

    def send_in(n):
        def copy(at, send_sem):
            plane, place = item_at(*at)
            return pltpu.make_async_remote_copy(
                src_ref=sent.at[n, rows(index_of(*at))],
                dst_ref=items.at[n, rows(place)],
                send_sem=send_sem,
                recv_sem=in_recv.at[n],
                device_id=device(at[0], plane, *at[1:]),
                device_id_type=MESH,
            )

        each_partner(lambda *at: copy(at, in_send.at[n]).start())

        @pl.when(local)
        def _():
            _, place = item_at(*here)
            pltpu.make_async_copy(
                sent.at[n, rows(mine)], items.at[n, rows(place)], in_recv.at[n]
            ).start()

        @pl.when(jnp.logical_not(local))
        def _():
            copy(here, own_send.at[n]).start()

    def send_out(n):
        def copy(at, send_sem):
            plane, place = owner_at(*at)
            return pltpu.make_async_remote_copy(
                src_ref=made.at[n, rows(place)],
                dst_ref=given.at[n, rows(mine)],
                send_sem=send_sem,
                recv_sem=out_recv.at[n],
                device_id=device(at[0], plane, *at[1:]),
                device_id_type=MESH,
            )

        each_partner(lambda *at: copy(at, out_send.at[n]).start())

        @pl.when(local)
        def _():
            _, place = owner_at(*here)
            pltpu.make_async_copy(
                made.at[n, rows(place)], given.at[n, rows(mine)], out_recv.at[n]
            ).start()

        @pl.when(jnp.logical_not(local))
        def _():
            copy(here, own_send.at[4 + n]).start()

    def arrived(buffer, sems, n):
        pltpu.make_async_copy(buffer.at[n], buffer.at[n], sems.at[n]).wait()

    def left(buffer, sems, n, own):
        most = buffer.at[n, pl.ds(0, T - ROWS)]
        pltpu.make_async_copy(most, most, sems.at[n]).wait()

        @pl.when(jnp.logical_not(local))
        def _():
            one = buffer.at[n, pl.ds(0, ROWS)]
            pltpu.make_async_copy(one, one, own_send.at[own]).wait()

    for n in range(4):
        by_head(n)
        if n == 0:
            pl.semaphore_wait(barrier, BLOCKS - local.astype(jnp.int32))
        send_in(n)

    q, k, v, g = (items.at[a] for a in range(4))
    o, dv, dq, dk = (made.at[a] for a in range(4))
    arrived(items, in_recv, 0)
    arrived(items, in_recv, 1)
    softmax_weights(q, k, scores, weights)
    k_t[...] = k[...].T
    arrived(items, in_recv, 2)
    v_t[...] = v[...].T
    attended(v_t, weights, o, out_wide)
    send_out(0)
    arrived(items, in_recv, 3)
    value_grads(weights, g, dv)
    send_out(1)
    row_dots(g, out_wide, row_dot)
    score_grads(weights, k_t, v, g, row_dot, ds, dq)
    send_out(2)
    key_grads(ds, q, dk)
    send_out(3)

    for n in range(4):
        left(sent, in_send, n, n)

    outputs = (o_out, dv_out, dq_out, dk_out)
    for n in range(4):
        arrived(given, out_recv, n)
        x = given[n].reshape(BLOCKS, ROWS, D)
        outputs[n][0] = jnp.swapaxes(x, 0, 1).reshape(ROWS, 2, H, D)
    for n in range(4):
        left(made, out_send, n, 4 + n)


def store_results(*refs):
    sems = refs[8]
    copies = [pltpu.make_async_copy(refs[a], refs[4 + a], sems.at[a]) for a in range(4)]
    for copy in copies:
        copy.start()
    for copy in copies:
        copy.wait()


def shards(queries, key_states, value_states, output_grad):
    in_vmem = pl.BlockSpec(memory_space=pltpu.VMEM)
    in_hbm = pl.BlockSpec(memory_space=pltpu.HBM)
    block = jax.ShapeDtypeStruct(queries.shape, jnp.bfloat16)
    low, wide = jnp.bfloat16, jnp.float32
    results = pl.pallas_call(
        kernel,
        out_shape=[pltpu.VMEM(queries.shape, low)] * 4,
        in_specs=[in_hbm] * 4,
        out_specs=[in_vmem] * 4,
        scratch_shapes=[
            pltpu.VMEM((4, ROWS, 2, H, D), low),
            pltpu.VMEM((4, T, D), low),
            pltpu.VMEM((4, T, D), low),
            pltpu.VMEM((4, T, D), low),
            pltpu.VMEM((4, T, D), low),
            pltpu.VMEM((T, TB), wide),
            pltpu.VMEM((T, T), low),
            pltpu.VMEM((T, T), low),
            pltpu.VMEM((D, T), low),
            pltpu.VMEM((D, T), low),
            pltpu.VMEM((T, D), wide),
            pltpu.VMEM((8, T), wide),
            pltpu.SemaphoreType.DMA((4,)),
            pltpu.SemaphoreType.DMA((4,)),
            pltpu.SemaphoreType.DMA((4,)),
            pltpu.SemaphoreType.DMA((4,)),
            pltpu.SemaphoreType.DMA((4,)),
            pltpu.SemaphoreType.DMA((8,)),
        ],
        compiler_params=pltpu.CompilerParams(
            collective_id=0, has_side_effects=True, vmem_limit_bytes=36 << 20
        ),
        cost_estimate=pl.CostEstimate(
            flops=12 * T * T * D // 2, bytes_accessed=16 * T * D, transcendentals=T * T // 2
        ),
        name="shifted_attention",
    )(*[
        pltpu.with_memory_space_constraint(x, pltpu.HBM)
        for x in (queries, key_states, value_states, output_grad)
    ])
    return tuple(
        pl.pallas_call(
            store_results,
            out_shape=[block] * 4,
            in_specs=[in_vmem] * 4,
            out_specs=[in_hbm] * 4,
            scratch_shapes=[pltpu.SemaphoreType.DMA((4,))],
            compiler_params=pltpu.CompilerParams(vmem_limit_bytes=4 << 20),
            name="store_results",
        )(*[pltpu.with_memory_space_constraint(x, pltpu.VMEM) for x in results])
    )


def solution(mesh):
    spec = P("ctx", ("seq", "head"), None, None, None)
    return jax.shard_map(
        shards, mesh=mesh, in_specs=(spec,) * 4, out_specs=(spec,) * 4, check_vma=False
    )
```

```python
import functools
import math

import jax
import jax.numpy as jnp
from jax import lax
from jax.experimental import pallas as pl
from jax.experimental.pallas import tpu as pltpu
from jax.sharding import PartitionSpec as P

H = 32
T = 2048
D = 128
BLOCKS = 64
ROWS = T // BLOCKS
TB = 256
NB = T // TB
SCALE = D**-0.5
EXP2_SCALE = SCALE * math.log2(math.e)
NT = (((1,), (1,)), ((), ()))
NN = (((1,), (0,)), ((), ()))
MESH = pl.DeviceIdType.MESH
DISTANCES = (4, 0, 3, 5, 2, 6, 1, 7)


def dot(a, b, dims=NN):
    return lax.dot_general(a, b, dims, preferred_element_type=jnp.float32)


def tile(i, n=1):
    return pl.ds(i * TB, n * TB)


def rows(block):
    return pl.ds(pl.multiple_of(block * ROWS, ROWS), ROWS)


def softmax_weights(q, k, scores, weights):
    for i in range(NB):
        q_tile = q[tile(i)]
        top = None
        for j in range(i + 1):
            s = dot(k[tile(j)], q_tile, NT)
            if j == i:
                key_pos = lax.broadcasted_iota(jnp.int32, (TB, TB), 0)
                query_pos = lax.broadcasted_iota(jnp.int32, (TB, TB), 1)
                s = jnp.where(key_pos <= query_pos, s, -jnp.inf)
            scores[tile(j)] = s
            part = jnp.max(s, axis=0, keepdims=True)
            top = part if top is None else jnp.maximum(top, part)
        shift = top * EXP2_SCALE
        total = None
        for j in range(i + 1):
            e = jnp.exp2(scores[tile(j)] * EXP2_SCALE - shift)
            scores[tile(j)] = e
            part = jnp.sum(e, axis=0, keepdims=True)
            total = part if total is None else total + part
        inverse = 1.0 / total
        for j in range(i + 1):
            weights[tile(j), tile(i)] = (scores[tile(j)] * inverse).astype(jnp.bfloat16)


def attended(v_t, weights, out, out_wide):
    for i in range(NB):
        o = dot(v_t[:, 0 : (i + 1) * TB], weights[0 : (i + 1) * TB, tile(i)]).T
        out_wide[tile(i)] = o
        out[tile(i)] = o.astype(jnp.bfloat16)


def value_grads(weights, g, dv):
    for j in range(NB):
        n = NB - j
        dv[tile(j)] = dot(weights[tile(j), tile(j, n)], g[tile(j, n)]).astype(jnp.bfloat16)


def row_dots(g, out_wide, row_dot):
    ones = jnp.ones((8, D), jnp.bfloat16)
    for i in range(NB):
        x = g[tile(i)].astype(jnp.float32) * out_wide[tile(i)]
        high = x.astype(jnp.bfloat16)
        low = (x - high.astype(jnp.float32)).astype(jnp.bfloat16)
        row_dot[:, tile(i)] = dot(ones, high, NT) + dot(ones, low, NT)


def score_grads(weights, k_t, v, g, row_dot, ds, dq):
    for i in range(NB):
        r = row_dot[0:1, tile(i)]
        for j in range(i + 1):
            dp = dot(v[tile(j)], g[tile(i)], NT)
            w = weights[tile(j), tile(i)].astype(jnp.float32)
            ds[tile(j), tile(i)] = (w * (dp - r)).astype(jnp.bfloat16)
        grad = dot(k_t[:, 0 : (i + 1) * TB], ds[0 : (i + 1) * TB, tile(i)])
        dq[tile(i)] = (grad * SCALE).T.astype(jnp.bfloat16)


def key_grads(ds, q, dk):
    for j in range(NB):
        n = NB - j
        dk[tile(j)] = (dot(ds[tile(j), tile(j, n)], q[tile(j, n)]) * SCALE).astype(jnp.bfloat16)


def by_position(x):
    return jnp.swapaxes(x.reshape(BLOCKS, ROWS, D), 0, 1).reshape(ROWS, 2, H, D)


def kernel(
    q_in, k_in, v_in, g_in, o_out, dq_out, dk_raw, dv_out,
    held, sent, items, made, given,
    scores, weights, ds, v_t, k_t, out_wide, row_dot,
    load_sem, in_send, in_recv, out_send, out_recv, own_send,
):
    seq = lax.axis_index("seq")
    ctx = lax.axis_index("ctx")
    head = lax.axis_index("head")
    me = seq * 32 + head
    z = head // 4
    high = (head // 2) % 2
    y = high * 2 + seq
    core = head % 2

    def device(seq2, plane, z2, high2, core2):
        return seq2, plane, z2 * 4 + high2 * 2 + core2


    def index_of(seq2, z2, high2, core2):
        return seq2 * H + core2 * (H // 2) + z2 * 2 + high2

    def neighbour(e):
        y2 = (y + e + 1) % 4
        return y2 % 2, y2 // 2, (core + 1 + e // 4) % 2

    def each_partner(visit):
        starts = [(z + dz) % 8 for dz in DISTANCES]

        def step(e, carry):
            seq2, high2, core2 = neighbour(e)
            for z2 in starts:
                visit(seq2, z2, high2, core2)
            return carry

        lax.fori_loop(0, 7, step, 0)
        for dz, z2 in zip(DISTANCES, starts):
            if dz:
                visit(seq, z2, high, core)

    def item_at(seq2, z2, high2, core2):
        return (ctx + 4 - core2 * (1 - seq)) % 4, (me + 32 * core2) % BLOCKS

    def owner_at(seq2, z2, high2, core2):
        block = seq2 * 32 + z2 * 4 + high2 * 2 + core2
        return (ctx + core * (1 - seq2)) % 4, (block + 32 * core) % BLOCKS

    mine = index_of(seq, z, high, core)
    local = core * (1 - seq) == 0
    here = (seq, z, high, core)

    barrier = pltpu.get_barrier_semaphore()

    def greet(*at):
        plane, _ = owner_at(*at)
        pl.semaphore_signal(
            barrier, inc=1, device_id=device(at[0], plane, *at[1:]), device_id_type=MESH
        )

    for e in range(8):
        seq2, high2, core2 = neighbour(e)
        for dz in DISTANCES:
            if (e, dz) != (7, 0):
                greet(seq2, (z + dz) % 8, high2, core2)

    @pl.when(jnp.logical_not(local))
    def _():
        greet(*here)

    inputs = (q_in, k_in, v_in, g_in)
    loads = [
        pltpu.make_async_copy(inputs[a].at[0], held.at[a], load_sem.at[a]) for a in range(4)
    ]
    for load in loads:
        load.start()

    def by_head(a):
        loads[a].wait()
        x = held[a].reshape(ROWS, BLOCKS, D)
        sent[a] = jnp.swapaxes(x, 0, 1).reshape(T, D)

    def send_in(n):
        def copy(at, send_sem):
            plane, place = item_at(*at)
            return pltpu.make_async_remote_copy(
                src_ref=sent.at[n, rows(index_of(*at))],
                dst_ref=items.at[n, rows(place)],
                send_sem=send_sem,
                recv_sem=in_recv.at[n],
                device_id=device(at[0], plane, *at[1:]),
                device_id_type=MESH,
            )

        each_partner(lambda *at: copy(at, in_send.at[n]).start())

        @pl.when(local)
        def _():
            _, place = item_at(*here)
            pltpu.make_async_copy(
                sent.at[n, rows(mine)], items.at[n, rows(place)], in_recv.at[n]
            ).start()

        @pl.when(jnp.logical_not(local))
        def _():
            copy(here, own_send.at[n]).start()

    def landing(n):
        return dk_raw if n == 3 else given.at[n]

    def send_out(n):
        def copy(at, send_sem):
            plane, place = owner_at(*at)
            return pltpu.make_async_remote_copy(
                src_ref=made.at[n, rows(place)],
                dst_ref=landing(n).at[rows(mine)],
                send_sem=send_sem,
                recv_sem=out_recv.at[n],
                device_id=device(at[0], plane, *at[1:]),
                device_id_type=MESH,
            )

        each_partner(lambda *at: copy(at, out_send.at[n]).start())

        @pl.when(local)
        def _():
            _, place = owner_at(*here)
            pltpu.make_async_copy(
                made.at[n, rows(place)], landing(n).at[rows(mine)], out_recv.at[n]
            ).start()

        @pl.when(jnp.logical_not(local))
        def _():
            copy(here, own_send.at[4 + n]).start()

    def arrived(whole, sem):
        pltpu.make_async_copy(whole, whole, sem).wait()

    def left(buffer, sems, n, own):
        most = buffer.at[n, pl.ds(0, T - ROWS)]
        pltpu.make_async_copy(most, most, sems.at[n]).wait()

        @pl.when(jnp.logical_not(local))
        def _():
            one = buffer.at[n, pl.ds(0, ROWS)]
            pltpu.make_async_copy(one, one, own_send.at[own]).wait()

    for n in range(4):
        by_head(n)
        if n == 0:
            pl.semaphore_wait(barrier, BLOCKS - local.astype(jnp.int32))
        send_in(n)

    q, k, v, g = (items.at[a] for a in range(4))
    o, dv, dq, dk = (made.at[a] for a in range(4))
    arrived(items.at[0], in_recv.at[0])
    arrived(items.at[1], in_recv.at[1])
    softmax_weights(q, k, scores, weights)
    k_t[...] = k[...].T
    arrived(items.at[2], in_recv.at[2])
    v_t[...] = v[...].T
    attended(v_t, weights, o, out_wide)
    send_out(0)
    arrived(items.at[3], in_recv.at[3])
    value_grads(weights, g, dv)
    send_out(1)
    row_dots(g, out_wide, row_dot)
    score_grads(weights, k_t, v, g, row_dot, ds, dq)
    send_out(2)
    key_grads(ds, q, dk)
    send_out(3)

    for n in range(4):
        left(sent, in_send, n, n)

    outputs = (o_out, dv_out, dq_out)
    for n in range(4):
        arrived(landing(n), out_recv.at[n])
        if n < 3:
            outputs[n][0] = by_position(given[n])
    for n in range(4):
        left(made, out_send, n, 4 + n)


def store_results(o, dq, dk_raw, dv, o_out, dq_out, dk_out, dv_out, dk, sems):
    pairs = ((o, o_out.at[0]), (dq, dq_out.at[0]), (dv, dv_out.at[0]), (dk, dk_out.at[0]))
    copies = [
        pltpu.make_async_copy(src if n == 3 else src.at[0], dst, sems.at[n])
        for n, (src, dst) in enumerate(pairs)
    ]
    for copy in copies[:3]:
        copy.start()
    dk[...] = by_position(dk_raw[...])
    copies[3].start()
    for copy in copies:
        copy.wait()


def shards(queries, key_states, value_states, output_grad):
    in_vmem = pl.BlockSpec(memory_space=pltpu.VMEM)
    in_hbm = pl.BlockSpec(memory_space=pltpu.HBM)
    block = jax.ShapeDtypeStruct(queries.shape, jnp.bfloat16)
    low, wide = jnp.bfloat16, jnp.float32
    results = pl.pallas_call(
        kernel,
        out_shape=[pltpu.VMEM(s, low) for s in (block.shape, block.shape, (T, D), block.shape)],
        in_specs=[in_hbm] * 4,
        out_specs=[in_vmem] * 4,
        scratch_shapes=[
            pltpu.VMEM((4, ROWS, 2, H, D), low),
            pltpu.VMEM((4, T, D), low),
            pltpu.VMEM((4, T, D), low),
            pltpu.VMEM((4, T, D), low),
            pltpu.VMEM((3, T, D), low),
            pltpu.VMEM((T, TB), wide),
            pltpu.VMEM((T, T), low),
            pltpu.VMEM((T, T), low),
            pltpu.VMEM((D, T), low),
            pltpu.VMEM((D, T), low),
            pltpu.VMEM((T, D), wide),
            pltpu.VMEM((8, T), wide),
            pltpu.SemaphoreType.DMA((4,)),
            pltpu.SemaphoreType.DMA((4,)),
            pltpu.SemaphoreType.DMA((4,)),
            pltpu.SemaphoreType.DMA((4,)),
            pltpu.SemaphoreType.DMA((4,)),
            pltpu.SemaphoreType.DMA((8,)),
        ],
        compiler_params=pltpu.CompilerParams(
            collective_id=0, has_side_effects=True, vmem_limit_bytes=36 << 20
        ),
        cost_estimate=pl.CostEstimate(
            flops=12 * T * T * D // 2, bytes_accessed=16 * T * D, transcendentals=T * T // 2
        ),
        name="shifted_attention",
    )(*[
        pltpu.with_memory_space_constraint(x, pltpu.HBM)
        for x in (queries, key_states, value_states, output_grad)
    ])
    return tuple(
        pl.pallas_call(
            store_results,
            out_shape=[block] * 4,
            in_specs=[in_vmem] * 4,
            out_specs=[in_hbm] * 4,
            scratch_shapes=[pltpu.VMEM((ROWS, 2, H, D), low), pltpu.SemaphoreType.DMA((4,))],
            compiler_params=pltpu.CompilerParams(vmem_limit_bytes=4 << 20),
            name="store_results",
        )(*[pltpu.with_memory_space_constraint(x, pltpu.VMEM) for x in results])
    )


def solution(mesh):
    spec = P("ctx", ("seq", "head"), None, None, None)
    return jax.shard_map(
        shards, mesh=mesh, in_specs=(spec,) * 4, out_specs=(spec,) * 4, check_vma=False
    )
```
